128 devices in a mesh: freq: 32 (over x, y, core), dm: 4 (over z).
Axes of the slice: x: 4, y: 4, z: 4, core: 2. Of those that a mesh axis runs over, the one named last changes fastest.
Arguments:
- voltages: bfloat16 [2, 1024, 245760], P(None, ('freq', 'dm')), may hold values from -6 to 6
- filter_weights: float32 [4, 16384], replicated, may hold values from -3 to 3
- beam_delay_index: int32 [512, 1024], replicated, may hold values from 0 to 16383
- delays: int32 [256, 16384], P(None, ('freq', 'dm')), may hold values from 0 to 8
- dm_counts: int32 [128], replicated, may hold values from 1 to 4, 256 in all
Outputs:
- dedispersed: float32 [512, 4, 512], P(('freq', 'dm'))
The draws below stay inside these ranges and needn't reach their ends.
Inputs may be any that keep to these rules, and one draw needn't show every extreme that they name: dm_counts sums to 256 and its largest entry is exactly 4.
All inputs are finite; a program needn't handle non-finite values.
Results may differ from the reference program's by a relative error of at most 0.0059.
Values may be sent and summed in bfloat16 or wider, within the bound.
A program may use at most 128 MiB of HBM per device.

```python
import math
from functools import partial
import jax
import jax.numpy as jnp
import numpy as np
from jax import lax

ANTENNA_COUNT = 1024
BEAM_COUNT = 512
CHANNEL_COUNT = 16384
TAPS = 4
MAXD = 8
SPECTRUM_COUNT = 12
SAMPLE_COUNT = 245760
OUT_T = 4
NDM = 256
MOST_DM = 4
SLOTS = 512
N_FREQ = 32
N_DM = 4


def plant(drawn, own_key, low, largest):
    spot = [jax.random.randint(jax.random.fold_in(own_key, axis), (), 0, length) for axis, length in enumerate(drawn.shape)]
    longest = drawn.shape.index(max(drawn.shape))
    neighbour = spot[:longest] + [(spot[longest] + 1) % drawn.shape[longest]] + spot[longest + 1:]
    return drawn.at[tuple(spot)].set(low).at[tuple(neighbour)].set(largest)


def steps_of(own_key, shape, cuts, low, top_value):
    def one(axis_at, parts):
        heights = jax.random.uniform(jax.random.fold_in(jax.random.fold_in(own_key, 6), axis_at), (parts,), jnp.float32, low / len(cuts), top_value / len(cuts))
        return jnp.repeat(jnp.exp(heights), shape[axis_at] // parts).reshape((-1,) + (1,) * (len(shape) - axis_at - 1))

    level = one(*cuts[0])
    for cut in cuts[1:]:
        level = level * one(*cut)
    return level


def length_profile(amount, total, bound, slope):
    loads = [(1 << 20) // math.isqrt(rank ** slope) + 1 for rank in range(2, amount + 1)]
    rest, counts = total - bound - (amount - 1), [1] * (amount - 1)
    while rest > 0:
        free = [i for i in range(amount - 1) if counts[i] < bound]
        whole, budget = sum([loads[i] for i in free]), rest
        for i in free:
            more = min(bound - counts[i], max(1, budget * loads[i] // whole), rest)
            counts[i] = counts[i] + more
            rest = rest - more
    return np.array([bound] + counts)


def uneven_parts(rng, number_of, total, limit, skew):
    if number_of == 2:
        one = jax.random.randint(rng, (), max(1, total - limit), min(limit, total - 1) + 1)
        return jnp.stack([one, total - one])
    tallies = jnp.asarray(length_profile(number_of, total, limit, skew), jnp.int32)
    couples = (number_of - 1) // 2
    donor, receiver = tallies[1:1 + 2 * couples:2], tallies[2:2 + 2 * couples:2]
    room = jnp.minimum(donor - 1, limit - receiver)
    moved = jax.random.randint(jax.random.fold_in(rng, 1), (couples,), 0, 1 << 20) % (room + 1)
    tallies = tallies.at[1:1 + 2 * couples:2].set(donor - moved).at[2:2 + 2 * couples:2].set(receiver + moved)
    return tallies[jax.random.permutation(jax.random.fold_in(rng, 2), number_of)]


def gaussian(rng, dims, scale, reach, shards=(), kind=jnp.bfloat16):
    drawn = scale * jax.random.normal(rng, dims, jnp.float32)
    if shards:
        drawn = drawn * steps_of(rng, dims, shards, -0.22, 0.18)
    return jnp.clip(drawn, -reach, reach).astype(kind)


def setup_inputs(seed: int = 0) -> dict:
    keys = jax.random.split(jax.random.key(seed), 6)
    return {
        "voltages": gaussian(keys[0], (2, ANTENNA_COUNT, SAMPLE_COUNT), 1.0, 6.0, ((1, 128),)),
        "filter_weights": gaussian(keys[1], (TAPS, CHANNEL_COUNT), 0.5, 3.0, (), jnp.float32),
        "beam_delay_index": plant(jax.random.randint(keys[2], (BEAM_COUNT, ANTENNA_COUNT), 0, CHANNEL_COUNT), jax.random.fold_in(keys[2], 1), 0, CHANNEL_COUNT - 1).astype(jnp.int32),
        "delays": plant(jax.random.randint(keys[3], (NDM, CHANNEL_COUNT), 0, MAXD + 1), jax.random.fold_in(keys[3], 1), 0, MAXD).astype(jnp.int32),
        "dm_counts": uneven_parts(keys[4], N_FREQ * N_DM, NDM, MOST_DM, 2).astype(jnp.int32),
    }


def channelize(filter_weights, block_volts):
    frame_rows = block_volts.astype(jnp.float32).reshape(2, block_volts.shape[1], SPECTRUM_COUNT + TAPS - 1, CHANNEL_COUNT)
    filter_output = filter_weights[0] * frame_rows[:, :, 0:SPECTRUM_COUNT]
    for tap_number in range(1, TAPS):
        filter_output = filter_output + filter_weights[tap_number] * frame_rows[:, :, tap_number:tap_number + SPECTRUM_COUNT]
    spectrum = jnp.fft.fft(lax.complex(filter_output[0], filter_output[1]), axis=-1) * (CHANNEL_COUNT ** -0.5)
    return jnp.stack([jnp.real(spectrum), jnp.imag(spectrum)]).astype(jnp.bfloat16)


def group_terms(beam_delay_index, spectrum_rows, delay_rows, group_id):
    channel_shard = spectrum_rows.shape[-1]
    centre = group_id * channel_shard + channel_shard // 2
    phases = ((beam_delay_index * centre) % CHANNEL_COUNT).astype(jnp.float32) * (2.0 * math.pi / CHANNEL_COUNT)
    weight_real = jnp.cos(phases).astype(jnp.bfloat16)
    weight_imaginary = (-jnp.sin(phases)).astype(jnp.bfloat16)
    spectrum_real = spectrum_rows[0].reshape(ANTENNA_COUNT, SPECTRUM_COUNT * channel_shard)
    spectrum_imaginary = spectrum_rows[1].reshape(ANTENNA_COUNT, SPECTRUM_COUNT * channel_shard)
    beam_real = (jnp.dot(weight_real, spectrum_real, preferred_element_type=jnp.float32) - jnp.dot(weight_imaginary, spectrum_imaginary, preferred_element_type=jnp.float32)) * (ANTENNA_COUNT ** -0.5)
    beam_imaginary = (jnp.dot(weight_real, spectrum_imaginary, preferred_element_type=jnp.float32) + jnp.dot(weight_imaginary, spectrum_real, preferred_element_type=jnp.float32)) * (ANTENNA_COUNT ** -0.5)
    power = (beam_real * beam_real + beam_imaginary * beam_imaginary).reshape(BEAM_COUNT, SPECTRUM_COUNT, channel_shard)
    centered = (power - jnp.mean(power, axis=1, keepdims=True)).astype(jnp.bfloat16)
    shifted = jnp.stack([centered[:, lag:lag + OUT_T, :] for lag in range(MAXD + 1)]).astype(jnp.float32)
    levels = jnp.arange(MAXD + 1, dtype=jnp.int32)
    onehot = (delay_rows[:, None, :] == levels[None, :, None]).astype(jnp.float32)
    return jnp.einsum('jdc,dbuc->jub', onehot, shifted)


def reference(voltages, filter_weights, beam_delay_index, delays, dm_counts):
    group_rows = N_FREQ * N_DM
    channel_shard = CHANNEL_COUNT // group_rows
    block_total = 16
    block_list = jnp.moveaxis(voltages.reshape(2, block_total, ANTENNA_COUNT // block_total, SAMPLE_COUNT), 1, 0)
    spectrum_rows = lax.map(partial(channelize, filter_weights), block_list)
    spectrum_rows = spectrum_rows.reshape(block_total, 2, ANTENNA_COUNT // block_total, SPECTRUM_COUNT, group_rows, channel_shard)
    spectrum_rows = jnp.transpose(spectrum_rows, (4, 1, 0, 2, 3, 5)).reshape(group_rows, 2, ANTENNA_COUNT, SPECTRUM_COUNT, channel_shard)
    delay_table = jnp.transpose(delays.reshape(NDM, group_rows, channel_shard), (1, 0, 2))

    def accumulate(running, pieces):
        spectra_group, delay_rows, group_id = pieces
        return running + group_terms(beam_delay_index, spectra_group, delay_rows, group_id), None

    running_init = jnp.zeros((NDM, OUT_T, BEAM_COUNT), jnp.float32)
    series, _ = lax.scan(accumulate, running_init, (spectrum_rows, delay_table, jnp.arange(group_rows, dtype=jnp.int32)))
    series = series * (CHANNEL_COUNT ** -0.5)
    offsets = (jnp.cumsum(dm_counts) - dm_counts).astype(jnp.int32)
    slot_ids = jnp.arange(SLOTS, dtype=jnp.int32)
    owners = slot_ids // MOST_DM
    within = slot_ids % MOST_DM
    trial_ids = jnp.clip(offsets[owners] + within, 0, NDM - 1).astype(jnp.int32)
    present = within < dm_counts[owners]
    return jnp.where(present[:, None, None], series[trial_ids], jnp.float32(0.0))
```

```python
import functools
import math

import jax
import jax.numpy as jnp
import ml_dtypes
import numpy as np
from jax import lax
from jax.experimental import pallas as pl
from jax.experimental.pallas import tpu as pltpu
from jax.sharding import PartitionSpec as P

MESH = pl.DeviceIdType.MESH
F32 = jnp.float32
BF16 = jnp.bfloat16

DEVICES = 128
CHIPS = 64
ANTENNAS = 8
SPECTRA = 12
TAPS = 4
FRAMES = SPECTRA + TAPS - 1
RADIX = 128
LENGTH = RADIX * RADIX
BEAMS = 512
TRIALS = 256
MOST_DM = 4
OUT_T = 4
GROUP = 2
ROWS = MOST_DM * OUT_T


def tables():
    ids = np.arange(RADIX)
    angle = 2.0 * np.pi * (np.outer(ids, ids) % RADIX) / RADIX
    dft = np.block([[np.cos(angle), np.sin(angle)], [-np.sin(angle), np.cos(angle)]])
    high = dft.astype(ml_dtypes.bfloat16)
    low = (dft - high.astype(np.float64)).astype(ml_dtypes.bfloat16)
    twist = 2.0 * np.pi * np.outer(ids, ids) / LENGTH
    scale = LENGTH**-0.5
    twist = np.concatenate([np.cos(twist) * scale, np.sin(twist) * scale]).astype(np.float32)
    return np.concatenate([high, high, low], axis=1), twist


def chip_orbits():
    far = lambda o: sum(min(v, 4 - v) for v in o)
    seen, orbits = set(), []
    for x in range(4):
        for y in range(4):
            for z in range(4):
                members = []
                for a, b, c in ((x, y, z), (y, z, x), (z, x, y)):
                    for sign in (1, -1):
                        member = (sign * a % 4, sign * b % 4, sign * c % 4)
                        if member not in members and member not in seen:
                            members.append(member)
                seen.update(members)
                if members:
                    orbits.append(members)
    orbits.sort(key=lambda m: -far(m[0]))
    return orbits


ORBITS = chip_orbits()
CHIP_ORDER = [o for m in ORBITS for o in m if o != (0, 0, 0)]
SEND_ORDER = [(o, c) for m in ORBITS for c in (0, 1) for o in m if (o, c) != ((0, 0, 0), 0)]


def position():
    freq, dm = lax.axis_index("freq"), lax.axis_index("dm")
    return freq // 8, (freq // 2) % 4, dm, freq % 2


def other(here, offset, core):
    x, y, z, c = here
    dx, dy, dz = offset
    return ((((x + dx) % 4) * 4 + (y + dy) % 4) * 2 + (c + core) % 2, (z + dz) % 4)


def index_of(device):
    return device[0] * 4 + device[1]


def halves(value):
    high = value.astype(BF16)
    return high, (value - high.astype(F32)).astype(BF16)


def body(
    volts, weights, beam_index, delays, counts, dft, twist, out,
    frames, taps, index, delay, count, dft_v, twist_v,
    filtered, first, second, turned_f32, sending, landed, steer, power, centered,
    hot, series, pair_send, pair_land, owner_send, owner_land,
    frame_sems, load_sems, own_sem, send_sem, land_sems, pair_sems, owner_sems,
):
    here = position()
    me = index_of((lax.axis_index("freq"), lax.axis_index("dm")))

    loads = [
        pltpu.make_async_copy(src, dst, load_sems.at[i])
        for i, (src, dst) in enumerate(
            [(weights, taps), (dft, dft_v), (twist, twist_v), (beam_index, index), (delays, delay), (counts, count)]
        )
    ]

    def frame_load(f):
        return pltpu.make_async_copy(
            volts.at[:, :, pl.ds(pl.multiple_of(f * LENGTH, LENGTH), LENGTH)], frames.at[f], frame_sems.at[f]
        )

    for f in range(TAPS):
        frame_load(f).start()
    for load in loads[:3]:
        load.start()
    for f in range(TAPS, FRAMES):
        frame_load(f).start()
    for load in loads[3:]:
        load.start()

    barrier = pltpu.get_barrier_semaphore()
    for offset, core in SEND_ORDER:
        pl.semaphore_signal(barrier, inc=1, device_id=other(here, offset, core), device_id_type=MESH)

    for load in loads[:3]:
        load.wait()
    for f in range(TAPS - 1):
        frame_load(f).wait()

    def channelize(s):
        frame_load(s + TAPS - 1).wait()
        wide = 1024

        def filter_part(part, _):
            at = pl.multiple_of(part * wide, wide)
            for p in range(2):
                total = taps[0:1, pl.ds(at, wide)] * frames[s, p, :, pl.ds(at, wide)].astype(F32)
                for k in range(1, TAPS):
                    total += taps[k : k + 1, pl.ds(at, wide)] * frames[s + k, p, :, pl.ds(at, wide)].astype(F32)
                for j in range(wide // RADIX):
                    row = p * RADIX * ANTENNAS + part * (wide // RADIX) * ANTENNAS + j * ANTENNAS
                    filtered[pl.ds(pl.multiple_of(row, ANTENNAS), ANTENNAS), :] = total[:, j * RADIX : (j + 1) * RADIX]
            return 0

        lax.fori_loop(0, LENGTH // wide, filter_part, 0)

        for pair in range(ANTENNAS // 2):
            for half in range(2):
                a = pair * 2 + half
                lanes = slice(half * RADIX, (half + 1) * RADIX)
                for p in range(2):
                    high, low = halves(filtered[pl.ds(p * RADIX * ANTENNAS + a, RADIX, stride=ANTENNAS), :])
                    first[pair, p * RADIX : (p + 1) * RADIX, lanes] = high
                    first[pair, (2 + p) * RADIX : (3 + p) * RADIX, lanes] = low
            part = jnp.dot(dft_v[:, 0:512], first[pair], preferred_element_type=F32)
            part += jnp.dot(dft_v[:, 512:768], first[pair, 0:256, :], preferred_element_type=F32)
            cos, sin = twist_v[0:RADIX, :], twist_v[RADIX:, :]
            for half in range(2):
                lanes = slice(half * RADIX, (half + 1) * RADIX)
                part_re, part_im = part[0:RADIX, lanes], part[RADIX:, lanes]
                for p, value in enumerate((part_re * cos + part_im * sin, part_im * cos - part_re * sin)):
                    high, low = halves(value)
                    rows = slice(half * RADIX, (half + 1) * RADIX)
                    second[pair, rows, p * RADIX : (p + 1) * RADIX] = high
                    second[pair, rows, (2 + p) * RADIX : (3 + p) * RADIX] = low
            contract = (((1,), (1,)), ((), ()))
            done = lax.dot_general(dft_v[:, 0:512], second[pair], contract, preferred_element_type=F32)
            done += lax.dot_general(dft_v[:, 512:768], second[pair, :, 0:256], contract, preferred_element_type=F32)
            for half in range(2):
                a = pair * 2 + half
                for p in range(2):
                    turned_f32[pl.ds(p * ANTENNAS + a, RADIX, stride=2 * ANTENNAS), :] = done[
                        p * RADIX : (p + 1) * RADIX, half * RADIX : (half + 1) * RADIX
                    ]
        sending[:, s] = turned_f32[...].reshape(DEVICES, 2 * ANTENNAS, RADIX).astype(BF16)

    def own_copy(group):
        span = pl.ds(group * GROUP, GROUP)
        return pltpu.make_async_copy(sending.at[me, span], landed.at[me, span], own_sem)

    def channelize_group(group, _):
        lax.fori_loop(0, GROUP, lambda i, _: (channelize(group * GROUP + i), 0)[1], 0)

        @pl.when(group == 0)
        def _():
            pl.semaphore_wait(barrier, DEVICES - 1)

        span = pl.ds(group * GROUP, GROUP)
        for offset, core in SEND_ORDER:
            device = other(here, offset, core)
            pltpu.make_async_remote_copy(
                src_ref=sending.at[index_of(device), span],
                dst_ref=landed.at[me, span],
                send_sem=send_sem,
                recv_sem=land_sems.at[group],
                device_id=device,
                device_id_type=MESH,
            ).start()
        copy = own_copy(group)
        copy.start()
        copy.wait()
        return 0

    lax.fori_loop(0, SPECTRA // GROUP, channelize_group, 0)

    loads[3].wait()
    centre = me * RADIX + RADIX // 2
    lane = lax.broadcasted_iota(jnp.int32, (RADIX, 256), 1)
    row = lax.broadcasted_iota(jnp.int32, (RADIX, 256), 0)
    spread = ((lane // 16) * 8 + lane % 8 == row).astype(F32).astype(BF16)
    quarter = ((lax.broadcasted_iota(jnp.int32, (64, 256), 1) // 8) % 2) * (LENGTH // 4)

    def steer_part(step, _):
        rows = pl.ds(pl.multiple_of((step // 8) * 64, 64), 64)
        block = step % 8
        found = index[rows, pl.ds(pl.multiple_of(block * RADIX, RADIX), RADIX)]
        high = (found >> 7).astype(F32).astype(BF16)
        low = (found & 127).astype(F32).astype(BF16)
        wide_high = jnp.dot(high, spread, preferred_element_type=F32)
        wide_low = jnp.dot(low, spread, preferred_element_type=F32)
        steps = (wide_high * 128.0 + wide_low).astype(jnp.int32)
        steps = (steps * centre - quarter) & (LENGTH - 1)
        turn = (steps + LENGTH // 8) >> 12
        x = (steps - (turn << 12)).astype(F32) * (2.0 * math.pi / LENGTH)
        y = x * x
        sin = x * (1.0 + y * (-1.0 / 6 + y * (1.0 / 120 + y * (-1.0 / 5040 + y * (1.0 / 362880)))))
        cos = 1.0 + y * (-0.5 + y * (1.0 / 24 + y * (-1.0 / 720 + y * (1.0 / 40320))))
        odd = (turn & 1) == 1
        cos_full = jnp.where(odd, sin, cos)
        sin_full = jnp.where(odd, cos, sin)
        cos_full = jnp.where(((turn + 1) & 2) == 2, -cos_full, cos_full)
        sin_full = jnp.where((turn & 2) == 2, -sin_full, sin_full)
        lanes = pl.ds(pl.multiple_of(block * 256, 256), 256)
        steer[rows, lanes] = cos_full.astype(BF16)
        steer[pl.ds(pl.multiple_of(BEAMS + (step // 8) * 64, 64), 64), lanes] = (-sin_full).astype(BF16)
        return 0

    lax.fori_loop(0, 64, steer_part, 0)

    loads[4].wait()
    loads[5].wait()
    more = (delay[...] + 1).astype(F32).astype(BF16)
    tally = count[...].astype(F32)
    x, y, z, c = here

    def hot_rows(block, owner):
        rows = lax.broadcasted_iota(jnp.int32, (ROWS, RADIX), 0)
        lanes = lax.broadcasted_iota(jnp.int32, (ROWS, RADIX), 1)
        before = jnp.sum(jnp.where(lanes < owner, tally, 0.0), axis=1, keepdims=True)
        mine = jnp.sum(jnp.where(lanes == owner, tally, 0.0), axis=1, keepdims=True)
        wide_rows = lax.broadcasted_iota(jnp.int32, (ROWS, TRIALS), 0)
        wide_lanes = lax.broadcasted_iota(jnp.int32, (ROWS, TRIALS), 1).astype(F32)
        within = (wide_rows // OUT_T).astype(F32)
        chosen = jnp.where((wide_lanes == before + within) & (within < mine), 1.0, 0.0).astype(BF16)
        level = jnp.dot(chosen, more, preferred_element_type=F32)
        level = jnp.where(level > 0.5, level + (rows % OUT_T).astype(F32) - 1.0, -1.0)
        for s in range(SPECTRA):
            hot[block * ROWS : (block + 1) * ROWS, s * RADIX : (s + 1) * RADIX] = jnp.where(
                level == float(s), 1.0, 0.0
            ).astype(BF16)

    for core in range(2):
        for i, offset in enumerate([(0, 0, 0)] + CHIP_ORDER):
            hot_rows(core * CHIPS + i, index_of(other(here, offset, core)))

    def beamform(group, _):
        span = pl.ds(group * GROUP, GROUP)
        arrived = landed.at[0 : DEVICES - 1, span]
        pltpu.make_async_copy(arrived, arrived, land_sems.at[group]).wait()
        spectra = jnp.concatenate(
            [landed[:, group * GROUP + i].reshape(DEVICES * 2 * ANTENNAS, RADIX) for i in range(GROUP)], axis=1
        )
        formed = jnp.dot(steer[...], spectra, preferred_element_type=F32)
        formed_re, formed_im = formed[:BEAMS], formed[BEAMS:]
        lanes = pl.ds(pl.multiple_of(group * GROUP * RADIX, GROUP * RADIX), GROUP * RADIX)
        power[:, lanes] = (formed_re * formed_re + formed_im * formed_im) * (1.0 / (DEVICES * ANTENNAS))
        return 0

    lax.fori_loop(0, SPECTRA // GROUP, beamform, 0)

    def centre_rows(step, _):
        rows = pl.ds(pl.multiple_of(step * 16, 16), 16)
        parts = [power[rows, s * RADIX : (s + 1) * RADIX] for s in range(SPECTRA)]
        mean = functools.reduce(lambda a, b: a + b, parts) * (1.0 / SPECTRA)
        for s, part in enumerate(parts):
            centered[rows, s * RADIX : (s + 1) * RADIX] = (part - mean).astype(BF16)
        return 0

    lax.fori_loop(0, BEAMS // 16, centre_rows, 0)

    contract = (((1,), (1,)), ((), ()))
    scale = LENGTH**-0.5
    half_rows = CHIPS * ROWS
    pair_send[...] = (
        lax.dot_general(hot[half_rows:, :], centered[...], contract, preferred_element_type=F32) * scale
    ).astype(BF16)
    pair = pltpu.make_async_remote_copy(
        src_ref=pair_send, dst_ref=pair_land, send_sem=pair_sems.at[0], recv_sem=pair_sems.at[1],
        device_id=other(here, (0, 0, 0), 1), device_id_type=MESH,
    )
    pair.start()
    series[...] = lax.dot_general(hot[0:half_rows, :], centered[...], contract, preferred_element_type=F32) * scale
    pair.wait()
    owner_send[...] = (series[ROWS:, :] + pair_land[ROWS:, :].astype(F32)).astype(BF16).reshape(CHIPS - 1, ROWS, BEAMS)
    for i, offset in enumerate(CHIP_ORDER):
        pltpu.make_async_remote_copy(
            src_ref=owner_send.at[i], dst_ref=owner_land.at[i], send_sem=owner_sems.at[0], recv_sem=owner_sems.at[1],
            device_id=other(here, offset, 0), device_id_type=MESH,
        ).start()
    total = series[0:ROWS, :] + pair_land[0:ROWS, :].astype(F32)
    pltpu.make_async_copy(owner_land, owner_land, owner_sems.at[1]).wait()
    total = lax.fori_loop(0, CHIPS - 1, lambda i, t: t + owner_land[i].astype(F32), total)
    for r in range(MOST_DM):
        out[r] = total[r * OUT_T : (r + 1) * OUT_T, :]

    pltpu.make_async_copy(owner_send, owner_send, owner_sems.at[0]).wait()
    gone = sending.at[0 : DEVICES - 1]
    pltpu.make_async_copy(gone, gone, send_sem).wait()


def local(voltages, filter_weights, beam_delay_index, delays, dm_counts):
    dft, twist = tables()
    anywhere = pl.BlockSpec(memory_space=pl.ANY)
    groups = SPECTRA // GROUP
    return pl.pallas_call(
        body,
        out_shape=jax.ShapeDtypeStruct((MOST_DM, OUT_T, BEAMS), F32),
        in_specs=[anywhere] * 7,
        out_specs=pl.BlockSpec(memory_space=pltpu.VMEM),
        scratch_shapes=[
            pltpu.VMEM((FRAMES, 2, ANTENNAS, LENGTH), BF16),
            pltpu.VMEM((TAPS, LENGTH), F32),
            pltpu.VMEM((BEAMS, DEVICES * ANTENNAS), jnp.int32),
            pltpu.VMEM((TRIALS, RADIX), jnp.int32),
            pltpu.VMEM((1, DEVICES), jnp.int32),
            pltpu.VMEM((256, 768), BF16),
            pltpu.VMEM((256, RADIX), F32),
            pltpu.VMEM((2 * RADIX * ANTENNAS, RADIX), F32),
            pltpu.VMEM((ANTENNAS // 2, 512, 256), BF16),
            pltpu.VMEM((ANTENNAS // 2, 256, 512), BF16),
            pltpu.VMEM((2 * RADIX * ANTENNAS, RADIX), F32),
            pltpu.VMEM((DEVICES, SPECTRA, 2 * ANTENNAS, RADIX), BF16),
            pltpu.VMEM((DEVICES, SPECTRA, 2 * ANTENNAS, RADIX), BF16),
            pltpu.VMEM((2 * BEAMS, DEVICES * 2 * ANTENNAS), BF16),
            pltpu.VMEM((BEAMS, SPECTRA * RADIX), F32),
            pltpu.VMEM((BEAMS, SPECTRA * RADIX), BF16),
            pltpu.VMEM((DEVICES * ROWS, SPECTRA * RADIX), BF16),
            pltpu.VMEM((CHIPS * ROWS, BEAMS), F32),
            pltpu.VMEM((CHIPS * ROWS, BEAMS), BF16),
            pltpu.VMEM((CHIPS * ROWS, BEAMS), BF16),
            pltpu.VMEM((CHIPS - 1, ROWS, BEAMS), BF16),
            pltpu.VMEM((CHIPS - 1, ROWS, BEAMS), BF16),
            pltpu.SemaphoreType.DMA((FRAMES,)),
            pltpu.SemaphoreType.DMA((6,)),
            pltpu.SemaphoreType.DMA,
            pltpu.SemaphoreType.DMA,
            pltpu.SemaphoreType.DMA((groups,)),
            pltpu.SemaphoreType.DMA((2,)),
            pltpu.SemaphoreType.DMA((2,)),
        ],
        compiler_params=pltpu.CompilerParams(
            collective_id=0, has_side_effects=True, vmem_limit_bytes=62 << 20
        ),
        cost_estimate=pl.CostEstimate(flops=16_000_000_000, bytes_accessed=12_000_000, transcendentals=0),
        name="channelize_turn_beamform",
    )(voltages, filter_weights, beam_delay_index, delays, dm_counts.reshape(1, DEVICES), dft, twist)


def solution(mesh):
    in_specs = (P(None, ("freq", "dm"), None), P(), P(), P(None, ("freq", "dm")), P())
    out_specs = P(("freq", "dm"), None, None)
    return jax.shard_map(local, mesh=mesh, in_specs=in_specs, out_specs=out_specs, check_vma=False)
```

```python
import functools
import math

import jax
import jax.numpy as jnp
import ml_dtypes
import numpy as np
from jax import lax
from jax.experimental import pallas as pl
from jax.experimental.pallas import tpu as pltpu
from jax.sharding import PartitionSpec as P

MESH = pl.DeviceIdType.MESH
F32 = jnp.float32
BF16 = jnp.bfloat16

DEVICES = 128
CHIPS = 64
ANTENNAS = 8
SPECTRA = 12
TAPS = 4
FRAMES = SPECTRA + TAPS - 1
RADIX = 128
LENGTH = RADIX * RADIX
BEAMS = 512
TRIALS = 256
MOST_DM = 4
OUT_T = 4
GROUP = 2
TILES = BEAMS // RADIX
ROWS = MOST_DM * OUT_T


def tables():
    ids = np.arange(RADIX)
    angle = 2.0 * np.pi * (np.outer(ids, ids) % RADIX) / RADIX
    dft = np.block([[np.cos(angle), np.sin(angle)], [-np.sin(angle), np.cos(angle)]])
    high = dft.astype(ml_dtypes.bfloat16)
    low = (dft - high.astype(np.float64)).astype(ml_dtypes.bfloat16)
    twist = 2.0 * np.pi * np.outer(ids, ids) / LENGTH
    scale = LENGTH**-0.5
    twist = np.concatenate([np.cos(twist) * scale, np.sin(twist) * scale]).astype(np.float32)
    return np.concatenate([high, high, low], axis=1), twist


def chip_orbits():
    far = lambda o: sum(min(v, 4 - v) for v in o)
    seen, orbits = set(), []
    for x in range(4):
        for y in range(4):
            for z in range(4):
                members = []
                for a, b, c in ((x, y, z), (y, z, x), (z, x, y)):
                    for sign in (1, -1):
                        member = (sign * a % 4, sign * b % 4, sign * c % 4)
                        if member not in members and member not in seen:
                            members.append(member)
                seen.update(members)
                if members:
                    orbits.append(members)
    orbits.sort(key=lambda m: -far(m[0]))
    return orbits


ORBITS = chip_orbits()
CHIP_ORDER = [o for m in ORBITS for o in m if o != (0, 0, 0)]
SEND_ORDER = [(o, c) for m in ORBITS for c in (0, 1) for o in m if (o, c) != ((0, 0, 0), 0)]


def position():
    freq, dm = lax.axis_index("freq"), lax.axis_index("dm")
    return freq // 8, (freq // 2) % 4, dm, freq % 2


def other(here, offset, core):
    x, y, z, c = here
    dx, dy, dz = offset
    return ((((x + dx) % 4) * 4 + (y + dy) % 4) * 2 + (c + core) % 2, (z + dz) % 4)


def index_of(device):
    return device[0] * 4 + device[1]


def halves(value):
    high = value.astype(BF16)
    return high, (value - high.astype(F32)).astype(BF16)


def body(
    volts, weights, beam_index, delays, counts, dft, twist, out,
    frames, taps, index, delay, count, dft_v, twist_v,
    filtered, first, second, turned_f32, sending, landed, steer, level_sum, level, centered,
    hot, series, pair_send, pair_land, owner_own, owner_send, owner_land,
    frame_sems, load_sems, send_sem, land_sems, pair_sems, owner_sems,
):
    here = position()
    me = index_of((lax.axis_index("freq"), lax.axis_index("dm")))

    loads = [
        pltpu.make_async_copy(src, dst, load_sems.at[i])
        for i, (src, dst) in enumerate(
            [(weights, taps), (dft, dft_v), (twist, twist_v), (beam_index, index), (delays, delay), (counts, count)]
        )
    ]

    def frame_load(f):
        return pltpu.make_async_copy(
            volts.at[:, :, pl.ds(pl.multiple_of(f * LENGTH, LENGTH), LENGTH)], frames.at[f], frame_sems.at[f]
        )

    for f in range(TAPS):
        frame_load(f).start()
    for load in loads[:3]:
        load.start()
    for f in range(TAPS, FRAMES):
        frame_load(f).start()
    for load in loads[3:]:
        load.start()

    barrier = pltpu.get_barrier_semaphore()
    for offset, core in SEND_ORDER:
        pl.semaphore_signal(barrier, inc=1, device_id=other(here, offset, core), device_id_type=MESH)

    for load in loads[:3]:
        load.wait()
    for f in range(TAPS - 1):
        frame_load(f).wait()

    def channelize(s):
        frame_load(s + TAPS - 1).wait()
        wide = 1024

        def filter_part(part, _):
            at = pl.multiple_of(part * wide, wide)
            for p in range(2):
                total = taps[0:1, pl.ds(at, wide)] * frames[s, p, :, pl.ds(at, wide)].astype(F32)
                for k in range(1, TAPS):
                    total += taps[k : k + 1, pl.ds(at, wide)] * frames[s + k, p, :, pl.ds(at, wide)].astype(F32)
                for j in range(wide // RADIX):
                    row = p * RADIX * ANTENNAS + part * (wide // RADIX) * ANTENNAS + j * ANTENNAS
                    filtered[pl.ds(pl.multiple_of(row, ANTENNAS), ANTENNAS), :] = total[:, j * RADIX : (j + 1) * RADIX]
            return 0

        lax.fori_loop(0, LENGTH // wide, filter_part, 0)

        for pair in range(ANTENNAS // 2):
            for half in range(2):
                a = pair * 2 + half
                lanes = slice(half * RADIX, (half + 1) * RADIX)
                for p in range(2):
                    high, low = halves(filtered[pl.ds(p * RADIX * ANTENNAS + a, RADIX, stride=ANTENNAS), :])
                    first[pair, p * RADIX : (p + 1) * RADIX, lanes] = high
                    first[pair, (2 + p) * RADIX : (3 + p) * RADIX, lanes] = low
            part = jnp.dot(dft_v[:, 0:512], first[pair], preferred_element_type=F32)
            part += jnp.dot(dft_v[:, 512:768], first[pair, 0:256, :], preferred_element_type=F32)
            cos, sin = twist_v[0:RADIX, :], twist_v[RADIX:, :]
            for half in range(2):
                lanes = slice(half * RADIX, (half + 1) * RADIX)
                part_re, part_im = part[0:RADIX, lanes], part[RADIX:, lanes]
                for p, value in enumerate((part_re * cos + part_im * sin, part_im * cos - part_re * sin)):
                    high, low = halves(value)
                    rows = slice(half * RADIX, (half + 1) * RADIX)
                    second[pair, rows, p * RADIX : (p + 1) * RADIX] = high
                    second[pair, rows, (2 + p) * RADIX : (3 + p) * RADIX] = low
            contract = (((1,), (1,)), ((), ()))
            done = lax.dot_general(dft_v[:, 0:512], second[pair], contract, preferred_element_type=F32)
            done += lax.dot_general(dft_v[:, 512:768], second[pair, :, 0:256], contract, preferred_element_type=F32)
            for half in range(2):
                a = pair * 2 + half
                for p in range(2):
                    turned_f32[pl.ds(p * ANTENNAS + a, RADIX, stride=2 * ANTENNAS), :] = done[
                        p * RADIX : (p + 1) * RADIX, half * RADIX : (half + 1) * RADIX
                    ]
        sending[:, s] = turned_f32[...].reshape(DEVICES, 2 * ANTENNAS, RADIX).astype(BF16)

    def channelize_and_send(s, _):
        channelize(s)

        @pl.when(s == 0)
        def _():
            pl.semaphore_wait(barrier, DEVICES - 1)

        for offset, core in SEND_ORDER:
            device = other(here, offset, core)
            pltpu.make_async_remote_copy(
                src_ref=sending.at[index_of(device), s],
                dst_ref=landed.at[me, s],
                send_sem=send_sem,
                recv_sem=land_sems.at[s],
                device_id=device,
                device_id_type=MESH,
            ).start()
        landed[me, s] = sending[me, s]
        return 0

    lax.fori_loop(0, SPECTRA, channelize_and_send, 0)

    loads[3].wait()
    centre = me * RADIX + RADIX // 2
    lane = lax.broadcasted_iota(jnp.int32, (RADIX, 256), 1)
    row = lax.broadcasted_iota(jnp.int32, (RADIX, 256), 0)
    spread = ((lane // 16) * 8 + lane % 8 == row).astype(F32).astype(BF16)
    quarter = ((lax.broadcasted_iota(jnp.int32, (64, 256), 1) // 8) % 2) * (LENGTH // 4)

    def steer_part(step, _):
        rows = pl.ds(pl.multiple_of((step // 8) * 64, 64), 64)
        block = step % 8
        found = index[rows, pl.ds(pl.multiple_of(block * RADIX, RADIX), RADIX)]
        high = (found >> 7).astype(F32).astype(BF16)
        low = (found & 127).astype(F32).astype(BF16)
        wide_high = jnp.dot(high, spread, preferred_element_type=F32)
        wide_low = jnp.dot(low, spread, preferred_element_type=F32)
        steps = (wide_high * 128.0 + wide_low).astype(jnp.int32)
        steps = (steps * centre - quarter) & (LENGTH - 1)
        turn = (steps + LENGTH // 8) >> 12
        x = (steps - (turn << 12)).astype(F32) * (2.0 * math.pi / LENGTH)
        y = x * x
        sin = x * (1.0 + y * (-1.0 / 6 + y * (1.0 / 120 + y * (-1.0 / 5040 + y * (1.0 / 362880)))))
        cos = 1.0 + y * (-0.5 + y * (1.0 / 24 + y * (-1.0 / 720 + y * (1.0 / 40320))))
        odd = (turn & 1) == 1
        cos_full = jnp.where(odd, sin, cos)
        sin_full = jnp.where(odd, cos, sin)
        cos_full = jnp.where(((turn + 1) & 2) == 2, -cos_full, cos_full)
        sin_full = jnp.where((turn & 2) == 2, -sin_full, sin_full)
        lanes = pl.ds(pl.multiple_of(block * 256, 256), 256)
        steer[rows, lanes] = cos_full.astype(BF16)
        steer[pl.ds(pl.multiple_of(BEAMS + (step // 8) * 64, 64), 64), lanes] = (-sin_full).astype(BF16)
        return 0

    lax.fori_loop(0, 64, steer_part, 0)

    loads[4].wait()
    loads[5].wait()
    more = (delay[...] + 1).astype(F32).astype(BF16)
    tally = count[...].astype(F32)
    x, y, z, c = here

    scale = LENGTH**-0.5

    def hot_rows(block, owner):
        rows = lax.broadcasted_iota(jnp.int32, (ROWS, RADIX), 0)
        lanes = lax.broadcasted_iota(jnp.int32, (ROWS, RADIX), 1)
        before = jnp.sum(jnp.where(lanes < owner, tally, 0.0), axis=1, keepdims=True)
        mine = jnp.sum(jnp.where(lanes == owner, tally, 0.0), axis=1, keepdims=True)
        wide_rows = lax.broadcasted_iota(jnp.int32, (ROWS, TRIALS), 0)
        wide_lanes = lax.broadcasted_iota(jnp.int32, (ROWS, TRIALS), 1).astype(F32)
        within = (wide_rows // OUT_T).astype(F32)
        chosen = jnp.where((wide_lanes == before + within) & (within < mine), 1.0, 0.0).astype(BF16)
        late = jnp.dot(chosen, more, preferred_element_type=F32)
        late = jnp.where(late > 0.5, late + (rows % OUT_T).astype(F32) - 1.0, -1.0)
        for s in range(SPECTRA):
            hot[block * ROWS : (block + 1) * ROWS, s * RADIX : (s + 1) * RADIX] = jnp.where(
                late == float(s), scale, 0.0
            ).astype(BF16)
        hot[block * ROWS : (block + 1) * ROWS, SPECTRA * RADIX :] = jnp.where(late >= 0.0, scale, 0.0).astype(BF16)

    for core in range(2):
        for i, offset in enumerate([(0, 0, 0)] + CHIP_ORDER):
            hot_rows(core * CHIPS + i, index_of(other(here, offset, core)))

    contract = (((1,), (1,)), ((), ()))
    half_rows = CHIPS * ROWS
    block_rows = 256
    level_sum[...] = jnp.zeros_like(level_sum)
    level[...] = jnp.zeros_like(level)
    series[...] = jnp.zeros_like(series)

    def beamform(group, _):
        for i in range(GROUP):
            arrived = landed.at[0 : DEVICES - 1, group * GROUP + i]
            pltpu.make_async_copy(arrived, arrived, land_sems.at[group * GROUP + i]).wait()
        spectra = jnp.concatenate(
            [landed[:, group * GROUP + i].reshape(DEVICES * 2 * ANTENNAS, RADIX) for i in range(GROUP)], axis=1
        )
        formed = jnp.dot(steer[...], spectra, preferred_element_type=F32)
        formed_re, formed_im = formed[:BEAMS], formed[BEAMS:]
        power = (formed_re * formed_re + formed_im * formed_im) * (1.0 / (DEVICES * ANTENNAS))
        both = power[:, :RADIX] + power[:, RADIX:]
        base = jnp.where(group == 0, both * (1.0 / GROUP), level[...])
        level[...] = base
        level_sum[...] += both
        for i in range(GROUP):
            at = pl.ds(pl.multiple_of((group * GROUP + i) * RADIX, RADIX), RADIX)
            centered[:, at] = (power[:, i * RADIX : (i + 1) * RADIX] - base).astype(BF16)

        @pl.when(group < SPECTRA // GROUP - 1)
        def _():
            at = pl.ds(pl.multiple_of(group * GROUP * RADIX, GROUP * RADIX), GROUP * RADIX)

            def add_rows(step, _):
                rows = pl.ds(pl.multiple_of(step * block_rows, block_rows), block_rows)
                series[rows, :] += lax.dot_general(
                    hot[rows, at], centered[:, at], contract, preferred_element_type=F32
                )
                return 0

            lax.fori_loop(0, 2 * half_rows // block_rows, add_rows, 0)

        return 0

    lax.fori_loop(0, SPECTRA // GROUP, beamform, 0)
    centered[:, SPECTRA * RADIX :] = (level[...] - level_sum[...] * (1.0 / SPECTRA)).astype(BF16)

    def last_rows(rows, t):
        at = slice((SPECTRA - GROUP) * RADIX, (SPECTRA + 1) * RADIX)
        beams = slice(t * RADIX, (t + 1) * RADIX)
        return series[rows, beams] + lax.dot_general(
            hot[rows, at], centered[beams, at], contract, preferred_element_type=F32
        )

    def pair_copy(t):
        return pltpu.make_async_remote_copy(
            src_ref=pair_send.at[t], dst_ref=pair_land.at[t], send_sem=pair_sems.at[0, t], recv_sem=pair_sems.at[1, t],
            device_id=other(here, (0, 0, 0), 1), device_id_type=MESH,
        )

    for t in range(TILES):
        pair_send[t] = last_rows(slice(half_rows, 2 * half_rows), t).astype(BF16)
        pair_copy(t).start()
    for t in range(TILES):
        mine = last_rows(slice(0, half_rows), t)
        pair_copy(t).wait_recv()
        mine += pair_land[t].astype(F32)
        owner_own[t] = mine[0:ROWS, :]
        owner_send[t] = mine[ROWS:, :].astype(BF16).reshape(CHIPS - 1, ROWS, RADIX)
        for i, offset in enumerate(CHIP_ORDER):
            pltpu.make_async_remote_copy(
                src_ref=owner_send.at[t, i], dst_ref=owner_land.at[t, i],
                send_sem=owner_sems.at[0, t], recv_sem=owner_sems.at[1, t],
                device_id=other(here, offset, 0), device_id_type=MESH,
            ).start()
    for t in range(TILES):
        pltpu.make_async_copy(owner_land.at[t], owner_land.at[t], owner_sems.at[1, t]).wait()
        total = lax.fori_loop(0, CHIPS - 1, lambda i, total: total + owner_land[t, i].astype(F32), owner_own[t])
        for r in range(MOST_DM):
            out[r, :, t * RADIX : (t + 1) * RADIX] = total[r * OUT_T : (r + 1) * OUT_T, :]

    for t in range(TILES):
        pair_copy(t).wait_send()
        pltpu.make_async_copy(owner_send.at[t], owner_send.at[t], owner_sems.at[0, t]).wait()
    gone = sending.at[0 : DEVICES - 1]
    pltpu.make_async_copy(gone, gone, send_sem).wait()


def local(voltages, filter_weights, beam_delay_index, delays, dm_counts):
    dft, twist = tables()
    anywhere = pl.BlockSpec(memory_space=pl.ANY)
    return pl.pallas_call(
        body,
        out_shape=jax.ShapeDtypeStruct((MOST_DM, OUT_T, BEAMS), F32),
        in_specs=[anywhere] * 7,
        out_specs=pl.BlockSpec(memory_space=pltpu.VMEM),
        scratch_shapes=[
            pltpu.VMEM((FRAMES, 2, ANTENNAS, LENGTH), BF16),
            pltpu.VMEM((TAPS, LENGTH), F32),
            pltpu.VMEM((BEAMS, DEVICES * ANTENNAS), jnp.int32),
            pltpu.VMEM((TRIALS, RADIX), jnp.int32),
            pltpu.VMEM((1, DEVICES), jnp.int32),
            pltpu.VMEM((256, 768), BF16),
            pltpu.VMEM((256, RADIX), F32),
            pltpu.VMEM((2 * RADIX * ANTENNAS, RADIX), F32),
            pltpu.VMEM((ANTENNAS // 2, 512, 256), BF16),
            pltpu.VMEM((ANTENNAS // 2, 256, 512), BF16),
            pltpu.VMEM((2 * RADIX * ANTENNAS, RADIX), F32),
            pltpu.VMEM((DEVICES, SPECTRA, 2 * ANTENNAS, RADIX), BF16),
            pltpu.VMEM((DEVICES, SPECTRA, 2 * ANTENNAS, RADIX), BF16),
            pltpu.VMEM((2 * BEAMS, DEVICES * 2 * ANTENNAS), BF16),
            pltpu.VMEM((BEAMS, RADIX), F32),
            pltpu.VMEM((BEAMS, RADIX), F32),
            pltpu.VMEM((BEAMS, (SPECTRA + 1) * RADIX), BF16),
            pltpu.VMEM((DEVICES * ROWS, (SPECTRA + 1) * RADIX), BF16),
            pltpu.VMEM((DEVICES * ROWS, BEAMS), F32),
            pltpu.VMEM((TILES, CHIPS * ROWS, RADIX), BF16),
            pltpu.VMEM((TILES, CHIPS * ROWS, RADIX), BF16),
            pltpu.VMEM((TILES, ROWS, RADIX), F32),
            pltpu.VMEM((TILES, CHIPS - 1, ROWS, RADIX), BF16),
            pltpu.VMEM((TILES, CHIPS - 1, ROWS, RADIX), BF16),
            pltpu.SemaphoreType.DMA((FRAMES,)),
            pltpu.SemaphoreType.DMA((6,)),
            pltpu.SemaphoreType.DMA,
            pltpu.SemaphoreType.DMA((SPECTRA,)),
            pltpu.SemaphoreType.DMA((2, TILES)),
            pltpu.SemaphoreType.DMA((2, TILES)),
        ],
        compiler_params=pltpu.CompilerParams(
            collective_id=0, has_side_effects=True, vmem_limit_bytes=62 << 20
        ),
        cost_estimate=pl.CostEstimate(flops=16_000_000_000, bytes_accessed=12_000_000, transcendentals=0),
        name="channelize_turn_beamform",
    )(voltages, filter_weights, beam_delay_index, delays, dm_counts.reshape(1, DEVICES), dft, twist)


def solution(mesh):
    in_specs = (P(None, ("freq", "dm"), None), P(), P(), P(None, ("freq", "dm")), P())
    out_specs = P(("freq", "dm"), None, None)
    return jax.shard_map(local, mesh=mesh, in_specs=in_specs, out_specs=out_specs, check_vma=False)
```

```python
import functools
import math

import jax
import jax.numpy as jnp
import ml_dtypes
import numpy as np
from jax import lax
from jax.experimental import pallas as pl
from jax.experimental.pallas import tpu as pltpu
from jax.sharding import PartitionSpec as P

MESH = pl.DeviceIdType.MESH
F32 = jnp.float32
BF16 = jnp.bfloat16

DEVICES = 128
CHIPS = 64
ANTENNAS = 8
SPECTRA = 12
TAPS = 4
FRAMES = SPECTRA + TAPS - 1
RADIX = 128
LENGTH = RADIX * RADIX
BEAMS = 512
TRIALS = 256
MOST_DM = 4
OUT_T = 4
GROUP = 2
TILES = BEAMS // RADIX
ROWS = MOST_DM * OUT_T


def tables():
    ids = np.arange(RADIX)
    angle = 2.0 * np.pi * (np.outer(ids, ids) % RADIX) / RADIX
    dft = np.block([[np.cos(angle), np.sin(angle)], [-np.sin(angle), np.cos(angle)]])
    high = dft.astype(ml_dtypes.bfloat16)
    low = (dft - high.astype(np.float64)).astype(ml_dtypes.bfloat16)
    twist = 2.0 * np.pi * np.outer(ids, ids) / LENGTH
    scale = LENGTH**-0.5
    twist = np.concatenate([np.cos(twist) * scale, np.sin(twist) * scale]).astype(np.float32)
    return np.concatenate([high, high, low], axis=1), twist


def chip_orbits():
    far = lambda o: sum(min(v, 4 - v) for v in o)
    seen, orbits = set(), []
    for x in range(4):
        for y in range(4):
            for z in range(4):
                members = []
                for a, b, c in ((x, y, z), (y, z, x), (z, x, y)):
                    for sign in (1, -1):
                        member = (sign * a % 4, sign * b % 4, sign * c % 4)
                        if member not in members and member not in seen:
                            members.append(member)
                seen.update(members)
                if members:
                    orbits.append(members)
    orbits.sort(key=lambda m: -far(m[0]))
    return orbits


ORBITS = chip_orbits()
CHIP_ORDER = [o for m in ORBITS for o in m if o != (0, 0, 0)]
SEND_ORDER = [(o, c) for m in ORBITS for c in (0, 1) for o in m if (o, c) != ((0, 0, 0), 0)]


def position():
    freq, dm = lax.axis_index("freq"), lax.axis_index("dm")
    return freq // 8, (freq // 2) % 4, dm, freq % 2


def other(here, offset, core):
    x, y, z, c = here
    dx, dy, dz = offset
    return ((((x + dx) % 4) * 4 + (y + dy) % 4) * 2 + (c + core) % 2, (z + dz) % 4)


def index_of(device):
    return device[0] * 4 + device[1]


def halves(value):
    high = value.astype(BF16)
    return high, (value - high.astype(F32)).astype(BF16)


def body(
    volts, weights, beam_index, delays, counts, dft, twist, out,
    frames, taps, index, delay, count, dft_v, twist_v,
    filtered, first, second, turned_f32, sending, landed, steer, level_sum, level, centered,
    hot, series, pair_send, pair_land, owner_own, owner_send, owner_land,
    frame_sems, load_sems, send_sem, land_sems, pair_sems, owner_sems,
):
    here = position()
    me = index_of((lax.axis_index("freq"), lax.axis_index("dm")))

    barrier = pltpu.get_barrier_semaphore()
    for offset, core in SEND_ORDER:
        pl.semaphore_signal(barrier, inc=1, device_id=other(here, offset, core), device_id_type=MESH)

    loads = [
        pltpu.make_async_copy(src, dst, load_sems.at[i])
        for i, (src, dst) in enumerate(
            [(weights, taps), (dft, dft_v), (twist, twist_v), (beam_index, index), (delays, delay), (counts, count)]
        )
    ]

    def frame_load(f):
        return pltpu.make_async_copy(
            volts.at[:, :, pl.ds(pl.multiple_of(f * LENGTH, LENGTH), LENGTH)], frames.at[f], frame_sems.at[f]
        )

    for f in range(TAPS):
        frame_load(f).start()
    for load in loads[:3]:
        load.start()
    for f in range(TAPS, FRAMES):
        frame_load(f).start()
    for load in loads[3:]:
        load.start()

    for load in loads[:3]:
        load.wait()
    for f in range(TAPS - 1):
        frame_load(f).wait()

    def channelize(s):
        frame_load(s + TAPS - 1).wait()
        wide = 1024

        def filter_part(part, _):
            at = pl.multiple_of(part * wide, wide)
            for p in range(2):
                total = taps[0:1, pl.ds(at, wide)] * frames[s, p, :, pl.ds(at, wide)].astype(F32)
                for k in range(1, TAPS):
                    total += taps[k : k + 1, pl.ds(at, wide)] * frames[s + k, p, :, pl.ds(at, wide)].astype(F32)
                for j in range(wide // RADIX):
                    row = p * RADIX * ANTENNAS + part * (wide // RADIX) * ANTENNAS + j * ANTENNAS
                    filtered[pl.ds(pl.multiple_of(row, ANTENNAS), ANTENNAS), :] = total[:, j * RADIX : (j + 1) * RADIX]
            return 0

        lax.fori_loop(0, LENGTH // wide, filter_part, 0)

        for pair in range(ANTENNAS // 2):
            for half in range(2):
                a = pair * 2 + half
                lanes = slice(half * RADIX, (half + 1) * RADIX)
                for p in range(2):
                    high, low = halves(filtered[pl.ds(p * RADIX * ANTENNAS + a, RADIX, stride=ANTENNAS), :])
                    first[pair, p * RADIX : (p + 1) * RADIX, lanes] = high
                    first[pair, (2 + p) * RADIX : (3 + p) * RADIX, lanes] = low
            part = jnp.dot(dft_v[:, 0:512], first[pair], preferred_element_type=F32)
            part += jnp.dot(dft_v[:, 512:768], first[pair, 0:256, :], preferred_element_type=F32)
            cos, sin = twist_v[0:RADIX, :], twist_v[RADIX:, :]
            for half in range(2):
                lanes = slice(half * RADIX, (half + 1) * RADIX)
                part_re, part_im = part[0:RADIX, lanes], part[RADIX:, lanes]
                for p, value in enumerate((part_re * cos + part_im * sin, part_im * cos - part_re * sin)):
                    high, low = halves(value)
                    rows = slice(half * RADIX, (half + 1) * RADIX)
                    second[pair, rows, p * RADIX : (p + 1) * RADIX] = high
                    second[pair, rows, (2 + p) * RADIX : (3 + p) * RADIX] = low
            contract = (((1,), (1,)), ((), ()))
            done = lax.dot_general(dft_v[:, 0:512], second[pair], contract, preferred_element_type=F32)
            done += lax.dot_general(dft_v[:, 512:768], second[pair, :, 0:256], contract, preferred_element_type=F32)
            for half in range(2):
                a = pair * 2 + half
                for p in range(2):
                    turned_f32[pl.ds(p * ANTENNAS + a, RADIX, stride=2 * ANTENNAS), :] = done[
                        p * RADIX : (p + 1) * RADIX, half * RADIX : (half + 1) * RADIX
                    ]
        sending[:, s] = turned_f32[...].reshape(DEVICES, 2 * ANTENNAS, RADIX).astype(BF16)

    def channelize_and_send(s, _):
        channelize(s)

        @pl.when(s == 0)
        def _():
            pl.semaphore_wait(barrier, DEVICES - 1)

        for offset, core in SEND_ORDER:
            device = other(here, offset, core)
            pltpu.make_async_remote_copy(
                src_ref=sending.at[index_of(device), s],
                dst_ref=landed.at[me, s],
                send_sem=send_sem,
                recv_sem=land_sems.at[s],
                device_id=device,
                device_id_type=MESH,
            ).start()
        landed[me, s] = sending[me, s]
        return 0

    lax.fori_loop(0, SPECTRA, channelize_and_send, 0)

    loads[3].wait()
    centre = me * RADIX + RADIX // 2
    lane = lax.broadcasted_iota(jnp.int32, (RADIX, 256), 1)
    row = lax.broadcasted_iota(jnp.int32, (RADIX, 256), 0)
    spread = ((lane // 16) * 8 + lane % 8 == row).astype(F32).astype(BF16)
    quarter = ((lax.broadcasted_iota(jnp.int32, (64, 256), 1) // 8) % 2) * (LENGTH // 4)

    def steer_part(step, _):
        rows = pl.ds(pl.multiple_of((step // 8) * 64, 64), 64)
        block = step % 8
        found = index[rows, pl.ds(pl.multiple_of(block * RADIX, RADIX), RADIX)]
        high = (found >> 7).astype(F32).astype(BF16)
        low = (found & 127).astype(F32).astype(BF16)
        wide_high = jnp.dot(high, spread, preferred_element_type=F32)
        wide_low = jnp.dot(low, spread, preferred_element_type=F32)
        steps = (wide_high * 128.0 + wide_low).astype(jnp.int32)
        steps = (steps * centre - quarter) & (LENGTH - 1)
        turn = (steps + LENGTH // 8) >> 12
        x = (steps - (turn << 12)).astype(F32) * (2.0 * math.pi / LENGTH)
        y = x * x
        sin = x * (1.0 + y * (-1.0 / 6 + y * (1.0 / 120 + y * (-1.0 / 5040 + y * (1.0 / 362880)))))
        cos = 1.0 + y * (-0.5 + y * (1.0 / 24 + y * (-1.0 / 720 + y * (1.0 / 40320))))
        odd = (turn & 1) == 1
        cos_full = jnp.where(odd, sin, cos)
        sin_full = jnp.where(odd, cos, sin)
        cos_full = jnp.where(((turn + 1) & 2) == 2, -cos_full, cos_full)
        sin_full = jnp.where((turn & 2) == 2, -sin_full, sin_full)
        lanes = pl.ds(pl.multiple_of(block * 256, 256), 256)
        steer[rows, lanes] = cos_full.astype(BF16)
        steer[pl.ds(pl.multiple_of(BEAMS + (step // 8) * 64, 64), 64), lanes] = (-sin_full).astype(BF16)
        return 0

    lax.fori_loop(0, 64, steer_part, 0)

    loads[4].wait()
    loads[5].wait()
    more = (delay[...] + 1).astype(F32).astype(BF16)
    tally = count[...].astype(F32)
    x, y, z, c = here

    scale = LENGTH**-0.5

    def hot_rows(block, owner):
        rows = lax.broadcasted_iota(jnp.int32, (ROWS, RADIX), 0)
        lanes = lax.broadcasted_iota(jnp.int32, (ROWS, RADIX), 1)
        before = jnp.sum(jnp.where(lanes < owner, tally, 0.0), axis=1, keepdims=True)
        mine = jnp.sum(jnp.where(lanes == owner, tally, 0.0), axis=1, keepdims=True)
        wide_rows = lax.broadcasted_iota(jnp.int32, (ROWS, TRIALS), 0)
        wide_lanes = lax.broadcasted_iota(jnp.int32, (ROWS, TRIALS), 1).astype(F32)
        within = (wide_rows // OUT_T).astype(F32)
        chosen = jnp.where((wide_lanes == before + within) & (within < mine), 1.0, 0.0).astype(BF16)
        late = jnp.dot(chosen, more, preferred_element_type=F32)
        late = jnp.where(late > 0.5, late + (rows % OUT_T).astype(F32) - 1.0, -1.0)
        for s in range(SPECTRA):
            hot[block * ROWS : (block + 1) * ROWS, s * RADIX : (s + 1) * RADIX] = jnp.where(
                late == float(s), scale, 0.0
            ).astype(BF16)
        hot[block * ROWS : (block + 1) * ROWS, SPECTRA * RADIX :] = jnp.where(late >= 0.0, scale, 0.0).astype(BF16)

    for core in range(2):
        for i, offset in enumerate([(0, 0, 0)] + CHIP_ORDER):
            hot_rows(core * CHIPS + i, index_of(other(here, offset, core)))

    contract = (((1,), (1,)), ((), ()))
    half_rows = CHIPS * ROWS
    block_rows = 256
    level_sum[...] = jnp.zeros_like(level_sum)
    level[...] = jnp.zeros_like(level)
    series[...] = jnp.zeros_like(series)

    def land(group):
        for i in range(GROUP):
            arrived = landed.at[0 : DEVICES - 1, group * GROUP + i]
            pltpu.make_async_copy(arrived, arrived, land_sems.at[group * GROUP + i]).wait()

    def spectra_of(group):
        return jnp.concatenate(
            [landed[:, group * GROUP + i].reshape(DEVICES * 2 * ANTENNAS, RADIX) for i in range(GROUP)], axis=1
        )

    def power_of(formed_re, formed_im):
        return (formed_re * formed_re + formed_im * formed_im) * (1.0 / (DEVICES * ANTENNAS))

    def beamform(group, _):
        land(group)
        formed = jnp.dot(steer[...], spectra_of(group), preferred_element_type=F32)
        power = power_of(formed[:BEAMS], formed[BEAMS:])
        both = power[:, :RADIX] + power[:, RADIX:]
        base = jnp.where(group == 0, both * (1.0 / GROUP), level[...])
        level[...] = base
        level_sum[...] += both
        for i in range(GROUP):
            at = pl.ds(pl.multiple_of((group * GROUP + i) * RADIX, RADIX), RADIX)
            centered[:, at] = (power[:, i * RADIX : (i + 1) * RADIX] - base).astype(BF16)
        at = pl.ds(pl.multiple_of(group * GROUP * RADIX, GROUP * RADIX), GROUP * RADIX)

        def add_rows(step, _):
            rows = pl.ds(pl.multiple_of(step * block_rows, block_rows), block_rows)
            series[rows, :] += lax.dot_general(hot[rows, at], centered[:, at], contract, preferred_element_type=F32)
            return 0

        lax.fori_loop(0, 2 * half_rows // block_rows, add_rows, 0)
        return 0

    last_group = SPECTRA // GROUP - 1
    lax.fori_loop(0, last_group, beamform, 0)

    def last_beams(t):
        beams = slice(t * RADIX, (t + 1) * RADIX)
        spectra = spectra_of(last_group)
        power = power_of(
            jnp.dot(steer[t * RADIX : (t + 1) * RADIX, :], spectra, preferred_element_type=F32),
            jnp.dot(steer[BEAMS + t * RADIX : BEAMS + (t + 1) * RADIX, :], spectra, preferred_element_type=F32),
        )
        base = level[beams, :]
        total = level_sum[beams, :] + power[:, :RADIX] + power[:, RADIX:]
        for i in range(GROUP):
            s = last_group * GROUP + i
            centered[beams, s * RADIX : (s + 1) * RADIX] = (power[:, i * RADIX : (i + 1) * RADIX] - base).astype(BF16)
        centered[beams, SPECTRA * RADIX :] = (base - total * (1.0 / SPECTRA)).astype(BF16)

    def last_rows(rows, t):
        at = slice(last_group * GROUP * RADIX, (SPECTRA + 1) * RADIX)
        beams = slice(t * RADIX, (t + 1) * RADIX)
        return series[rows, beams] + lax.dot_general(
            hot[rows, at], centered[beams, at], contract, preferred_element_type=F32
        )

    def pair_copy(t):
        return pltpu.make_async_remote_copy(
            src_ref=pair_send.at[t], dst_ref=pair_land.at[t], send_sem=pair_sems.at[0, t], recv_sem=pair_sems.at[1, t],
            device_id=other(here, (0, 0, 0), 1), device_id_type=MESH,
        )

    def owners_out(t):
        pair_copy(t).wait_recv()
        mine = series[0:half_rows, t * RADIX : (t + 1) * RADIX] + pair_land[t].astype(F32)
        owner_own[t] = mine[0:ROWS, :]
        owner_send[t] = mine[ROWS:, :].astype(BF16).reshape(CHIPS - 1, ROWS, RADIX)
        for i, offset in enumerate(CHIP_ORDER):
            pltpu.make_async_remote_copy(
                src_ref=owner_send.at[t, i], dst_ref=owner_land.at[t, i],
                send_sem=owner_sems.at[0, t], recv_sem=owner_sems.at[1, t],
                device_id=other(here, offset, 0), device_id_type=MESH,
            ).start()

    land(last_group)
    for t in range(TILES):
        last_beams(t)
        pair_send[t] = last_rows(slice(half_rows, 2 * half_rows), t).astype(BF16)
        pair_copy(t).start()
        series[0:half_rows, t * RADIX : (t + 1) * RADIX] = last_rows(slice(0, half_rows), t)
        if t > 0:
            owners_out(t - 1)
    owners_out(TILES - 1)
    for t in range(TILES):
        pltpu.make_async_copy(owner_land.at[t], owner_land.at[t], owner_sems.at[1, t]).wait()
        totals = [owner_own[t], 0.0, 0.0, 0.0]
        for i in range(CHIPS - 1):
            totals[i % 4] += owner_land[t, i].astype(F32)
        total = (totals[0] + totals[1]) + (totals[2] + totals[3])
        for r in range(MOST_DM):
            out[r, :, t * RADIX : (t + 1) * RADIX] = total[r * OUT_T : (r + 1) * OUT_T, :]

    for t in range(TILES):
        pair_copy(t).wait_send()
        pltpu.make_async_copy(owner_send.at[t], owner_send.at[t], owner_sems.at[0, t]).wait()
    gone = sending.at[0 : DEVICES - 1]
    pltpu.make_async_copy(gone, gone, send_sem).wait()


def local(voltages, filter_weights, beam_delay_index, delays, dm_counts):
    dft, twist = tables()
    anywhere = pl.BlockSpec(memory_space=pl.ANY)
    return pl.pallas_call(
        body,
        out_shape=jax.ShapeDtypeStruct((MOST_DM, OUT_T, BEAMS), F32),
        in_specs=[anywhere] * 7,
        out_specs=pl.BlockSpec(memory_space=pltpu.VMEM),
        scratch_shapes=[
            pltpu.VMEM((FRAMES, 2, ANTENNAS, LENGTH), BF16),
            pltpu.VMEM((TAPS, LENGTH), F32),
            pltpu.VMEM((BEAMS, DEVICES * ANTENNAS), jnp.int32),
            pltpu.VMEM((TRIALS, RADIX), jnp.int32),
            pltpu.VMEM((1, DEVICES), jnp.int32),
            pltpu.VMEM((256, 768), BF16),
            pltpu.VMEM((256, RADIX), F32),
            pltpu.VMEM((2 * RADIX * ANTENNAS, RADIX), F32),
            pltpu.VMEM((ANTENNAS // 2, 512, 256), BF16),
            pltpu.VMEM((ANTENNAS // 2, 256, 512), BF16),
            pltpu.VMEM((2 * RADIX * ANTENNAS, RADIX), F32),
            pltpu.VMEM((DEVICES, SPECTRA, 2 * ANTENNAS, RADIX), BF16),
            pltpu.VMEM((DEVICES, SPECTRA, 2 * ANTENNAS, RADIX), BF16),
            pltpu.VMEM((2 * BEAMS, DEVICES * 2 * ANTENNAS), BF16),
            pltpu.VMEM((BEAMS, RADIX), F32),
            pltpu.VMEM((BEAMS, RADIX), F32),
            pltpu.VMEM((BEAMS, (SPECTRA + 1) * RADIX), BF16),
            pltpu.VMEM((DEVICES * ROWS, (SPECTRA + 1) * RADIX), BF16),
            pltpu.VMEM((DEVICES * ROWS, BEAMS), F32),
            pltpu.VMEM((TILES, CHIPS * ROWS, RADIX), BF16),
            pltpu.VMEM((TILES, CHIPS * ROWS, RADIX), BF16),
            pltpu.VMEM((TILES, ROWS, RADIX), F32),
            pltpu.VMEM((TILES, CHIPS - 1, ROWS, RADIX), BF16),
            pltpu.VMEM((TILES, CHIPS - 1, ROWS, RADIX), BF16),
            pltpu.SemaphoreType.DMA((FRAMES,)),
            pltpu.SemaphoreType.DMA((6,)),
            pltpu.SemaphoreType.DMA,
            pltpu.SemaphoreType.DMA((SPECTRA,)),
            pltpu.SemaphoreType.DMA((2, TILES)),
            pltpu.SemaphoreType.DMA((2, TILES)),
        ],
        compiler_params=pltpu.CompilerParams(
            collective_id=0, has_side_effects=True, vmem_limit_bytes=62 << 20
        ),
        cost_estimate=pl.CostEstimate(flops=16_000_000_000, bytes_accessed=12_000_000, transcendentals=0),
        name="channelize_turn_beamform",
    )(voltages, filter_weights, beam_delay_index, delays, dm_counts.reshape(1, DEVICES), dft, twist)


def solution(mesh):
    in_specs = (P(None, ("freq", "dm"), None), P(), P(), P(None, ("freq", "dm")), P())
    out_specs = P(("freq", "dm"), None, None)
    return jax.shard_map(local, mesh=mesh, in_specs=in_specs, out_specs=out_specs, check_vma=False)
```

```python
import functools
import math

import jax
import jax.numpy as jnp
import ml_dtypes
import numpy as np
from jax import lax
from jax.experimental import pallas as pl
from jax.experimental.pallas import tpu as pltpu
from jax.sharding import PartitionSpec as P

MESH = pl.DeviceIdType.MESH
F32 = jnp.float32
BF16 = jnp.bfloat16

DEVICES = 128
CHIPS = 64
ANTENNAS = 8
SPECTRA = 12
TAPS = 4
FRAMES = SPECTRA + TAPS - 1
RADIX = 128
LENGTH = RADIX * RADIX
BEAMS = 512
TRIALS = 256
MOST_DM = 4
OUT_T = 4
GROUP = 2
TILES = BEAMS // RADIX
ROWS = MOST_DM * OUT_T


def tables():
    ids = np.arange(RADIX)
    angle = 2.0 * np.pi * (np.outer(ids, ids) % RADIX) / RADIX
    dft = np.block([[np.cos(angle), np.sin(angle)], [-np.sin(angle), np.cos(angle)]])
    high = dft.astype(ml_dtypes.bfloat16)
    low = (dft - high.astype(np.float64)).astype(ml_dtypes.bfloat16)
    twist = 2.0 * np.pi * np.outer(ids, ids) / LENGTH
    scale = LENGTH**-0.5
    twist = np.concatenate([np.cos(twist) * scale, np.sin(twist) * scale]).astype(np.float32)
    return np.concatenate([high, high, low], axis=1), twist


def chip_orbits():
    far = lambda o: sum(min(v, 4 - v) for v in o)
    seen, orbits = set(), []
    for x in range(4):
        for y in range(4):
            for z in range(4):
                members = []
                for a, b, c in ((x, y, z), (y, z, x), (z, x, y)):
                    for sign in (1, -1):
                        member = (sign * a % 4, sign * b % 4, sign * c % 4)
                        if member not in members and member not in seen:
                            members.append(member)
                seen.update(members)
                if members:
                    orbits.append(members)
    orbits.sort(key=lambda m: -far(m[0]))
    return orbits


ORBITS = chip_orbits()
CHIP_ORDER = [o for m in ORBITS for o in m if o != (0, 0, 0)]
SEND_ORDER = [(o, c) for m in ORBITS for c in (0, 1) for o in m if (o, c) != ((0, 0, 0), 0)]


def position():
    freq, dm = lax.axis_index("freq"), lax.axis_index("dm")
    return freq // 8, (freq // 2) % 4, dm, freq % 2


def other(here, offset, core):
    x, y, z, c = here
    dx, dy, dz = offset
    return ((((x + dx) % 4) * 4 + (y + dy) % 4) * 2 + (c + core) % 2, (z + dz) % 4)


def index_of(device):
    return device[0] * 4 + device[1]


def halves(value):
    high = value.astype(BF16)
    return high, (value - high.astype(F32)).astype(BF16)


def body(
    volts, weights, beam_index, delays, counts, dft, twist, out,
    frames, taps, index, delay, count, dft_v, twist_v,
    filtered, first, second, turned_f32, sending, landed, steer, level_sum, level, centered,
    hot, series, pair_send, pair_land, owner_own, owner_send, owner_land,
    frame_sems, load_sems, send_sem, land_sems, pair_sems, owner_sems,
):
    here = position()
    me = index_of((lax.axis_index("freq"), lax.axis_index("dm")))

    barrier = pltpu.get_barrier_semaphore()
    for offset, core in SEND_ORDER:
        pl.semaphore_signal(barrier, inc=1, device_id=other(here, offset, core), device_id_type=MESH)

    loads = [
        pltpu.make_async_copy(src, dst, load_sems.at[i])
        for i, (src, dst) in enumerate(
            [(weights, taps), (dft, dft_v), (twist, twist_v), (beam_index, index), (delays, delay), (counts, count)]
        )
    ]

    def frame_load(f):
        return pltpu.make_async_copy(
            volts.at[:, :, pl.ds(pl.multiple_of(f * LENGTH, LENGTH), LENGTH)], frames.at[f], frame_sems.at[f]
        )

    for f in range(TAPS):
        frame_load(f).start()
    for load in loads[:3]:
        load.start()
    for f in range(TAPS, FRAMES):
        frame_load(f).start()
    for load in loads[3:]:
        load.start()

    for load in loads[:3]:
        load.wait()
    for f in range(TAPS - 1):
        frame_load(f).wait()

    def channelize(s):
        frame_load(s + TAPS - 1).wait()
        wide = 1024

        def filter_part(part, _):
            at = pl.multiple_of(part * wide, wide)
            for p in range(2):
                total = taps[0:1, pl.ds(at, wide)] * frames[s, p, :, pl.ds(at, wide)].astype(F32)
                for k in range(1, TAPS):
                    total += taps[k : k + 1, pl.ds(at, wide)] * frames[s + k, p, :, pl.ds(at, wide)].astype(F32)
                for j in range(wide // RADIX):
                    row = p * RADIX * ANTENNAS + part * (wide // RADIX) * ANTENNAS + j * ANTENNAS
                    filtered[pl.ds(pl.multiple_of(row, ANTENNAS), ANTENNAS), :] = total[:, j * RADIX : (j + 1) * RADIX]
            return 0

        lax.fori_loop(0, LENGTH // wide, filter_part, 0)

        for pair in range(ANTENNAS // 2):
            for half in range(2):
                a = pair * 2 + half
                lanes = slice(half * RADIX, (half + 1) * RADIX)
                for p in range(2):
                    high, low = halves(filtered[pl.ds(p * RADIX * ANTENNAS + a, RADIX, stride=ANTENNAS), :])
                    first[pair, p * RADIX : (p + 1) * RADIX, lanes] = high
                    first[pair, (2 + p) * RADIX : (3 + p) * RADIX, lanes] = low
            part = jnp.dot(dft_v[:, 0:512], first[pair], preferred_element_type=F32)
            part += jnp.dot(dft_v[:, 512:768], first[pair, 0:256, :], preferred_element_type=F32)
            cos, sin = twist_v[0:RADIX, :], twist_v[RADIX:, :]
            for half in range(2):
                lanes = slice(half * RADIX, (half + 1) * RADIX)
                part_re, part_im = part[0:RADIX, lanes], part[RADIX:, lanes]
                for p, value in enumerate((part_re * cos + part_im * sin, part_im * cos - part_re * sin)):
                    high, low = halves(value)
                    rows = slice(half * RADIX, (half + 1) * RADIX)
                    second[pair, rows, p * RADIX : (p + 1) * RADIX] = high
                    second[pair, rows, (2 + p) * RADIX : (3 + p) * RADIX] = low
            contract = (((1,), (1,)), ((), ()))
            done = lax.dot_general(dft_v[:, 0:512], second[pair], contract, preferred_element_type=F32)
            done += lax.dot_general(dft_v[:, 512:768], second[pair, :, 0:256], contract, preferred_element_type=F32)
            for half in range(2):
                a = pair * 2 + half
                for p in range(2):
                    turned_f32[pl.ds(p * ANTENNAS + a, RADIX, stride=2 * ANTENNAS), :] = done[
                        p * RADIX : (p + 1) * RADIX, half * RADIX : (half + 1) * RADIX
                    ]
        sending[:, s] = turned_f32[...].reshape(DEVICES, 2 * ANTENNAS, RADIX).astype(BF16)

    def channelize_and_send(s, _):
        channelize(s)

        @pl.when(s == 0)
        def _():
            pl.semaphore_wait(barrier, DEVICES - 1)

        for offset, core in SEND_ORDER:
            device = other(here, offset, core)
            pltpu.make_async_remote_copy(
                src_ref=sending.at[index_of(device), s],
                dst_ref=landed.at[me, s],
                send_sem=send_sem,
                recv_sem=land_sems.at[s],
                device_id=device,
                device_id_type=MESH,
            ).start()
        landed[me, s] = sending[me, s]
        return 0

    lax.fori_loop(0, SPECTRA, channelize_and_send, 0)

    loads[3].wait()
    centre = me * RADIX + RADIX // 2
    lane = lax.broadcasted_iota(jnp.int32, (RADIX, 256), 1)
    row = lax.broadcasted_iota(jnp.int32, (RADIX, 256), 0)
    spread = ((lane // 16) * 8 + lane % 8 == row).astype(F32).astype(BF16)
    quarter = ((lax.broadcasted_iota(jnp.int32, (64, 256), 1) // 8) % 2) * (LENGTH // 4)

    def steer_part(step, _):
        rows = pl.ds(pl.multiple_of((step // 8) * 64, 64), 64)
        block = step % 8
        found = index[rows, pl.ds(pl.multiple_of(block * RADIX, RADIX), RADIX)]
        high = (found >> 7).astype(F32).astype(BF16)
        low = (found & 127).astype(F32).astype(BF16)
        wide_high = jnp.dot(high, spread, preferred_element_type=F32)
        wide_low = jnp.dot(low, spread, preferred_element_type=F32)
        steps = (wide_high * 128.0 + wide_low).astype(jnp.int32)
        steps = (steps * centre - quarter) & (LENGTH - 1)
        turn = (steps + LENGTH // 8) >> 12
        x = (steps - (turn << 12)).astype(F32) * (2.0 * math.pi / LENGTH)
        y = x * x
        sin = x * (1.0 + y * (-1.0 / 6 + y * (1.0 / 120 + y * (-1.0 / 5040 + y * (1.0 / 362880)))))
        cos = 1.0 + y * (-0.5 + y * (1.0 / 24 + y * (-1.0 / 720 + y * (1.0 / 40320))))
        odd = (turn & 1) == 1
        cos_full = jnp.where(odd, sin, cos)
        sin_full = jnp.where(odd, cos, sin)
        cos_full = jnp.where(((turn + 1) & 2) == 2, -cos_full, cos_full)
        sin_full = jnp.where((turn & 2) == 2, -sin_full, sin_full)
        lanes = pl.ds(pl.multiple_of(block * 256, 256), 256)
        steer[rows, lanes] = cos_full.astype(BF16)
        steer[pl.ds(pl.multiple_of(BEAMS + (step // 8) * 64, 64), 64), lanes] = (-sin_full).astype(BF16)
        return 0

    lax.fori_loop(0, 64, steer_part, 0)

    loads[4].wait()
    loads[5].wait()
    more = (delay[...] + 1).astype(F32).astype(BF16)
    tally = count[...].astype(F32)
    x, y, z, c = here

    scale = LENGTH**-0.5

    def hot_rows(block, owner):
        rows = lax.broadcasted_iota(jnp.int32, (ROWS, RADIX), 0)
        lanes = lax.broadcasted_iota(jnp.int32, (ROWS, RADIX), 1)
        before = jnp.sum(jnp.where(lanes < owner, tally, 0.0), axis=1, keepdims=True)
        mine = jnp.sum(jnp.where(lanes == owner, tally, 0.0), axis=1, keepdims=True)
        wide_rows = lax.broadcasted_iota(jnp.int32, (ROWS, TRIALS), 0)
        wide_lanes = lax.broadcasted_iota(jnp.int32, (ROWS, TRIALS), 1).astype(F32)
        within = (wide_rows // OUT_T).astype(F32)
        chosen = jnp.where((wide_lanes == before + within) & (within < mine), 1.0, 0.0).astype(BF16)
        late = jnp.dot(chosen, more, preferred_element_type=F32)
        late = jnp.where(late > 0.5, late + (rows % OUT_T).astype(F32) - 1.0, -1.0)
        for s in range(SPECTRA):
            hot[block * ROWS : (block + 1) * ROWS, s * RADIX : (s + 1) * RADIX] = jnp.where(
                late == float(s), scale, 0.0
            ).astype(BF16)
        hot[block * ROWS : (block + 1) * ROWS, SPECTRA * RADIX :] = jnp.where(late >= 0.0, scale, 0.0).astype(BF16)

    for core in range(2):
        for i, offset in enumerate([(0, 0, 0)] + CHIP_ORDER):
            hot_rows(core * CHIPS + i, index_of(other(here, offset, core)))

    contract = (((1,), (1,)), ((), ()))
    half_rows = CHIPS * ROWS
    block_rows = 256
    level_sum[...] = jnp.zeros_like(level_sum)
    level[...] = jnp.zeros_like(level)
    series[...] = jnp.zeros_like(series)

    def land(group):
        for i in range(GROUP):
            arrived = landed.at[0 : DEVICES - 1, group * GROUP + i]
            pltpu.make_async_copy(arrived, arrived, land_sems.at[group * GROUP + i]).wait()

    def spectra_of(group):
        return jnp.concatenate(
            [landed[:, group * GROUP + i].reshape(DEVICES * 2 * ANTENNAS, RADIX) for i in range(GROUP)], axis=1
        )

    def power_of(formed_re, formed_im):
        return (formed_re * formed_re + formed_im * formed_im) * (1.0 / (DEVICES * ANTENNAS))

    def beamform(group, _):
        land(group)
        formed = jnp.dot(steer[...], spectra_of(group), preferred_element_type=F32)
        power = power_of(formed[:BEAMS], formed[BEAMS:])
        both = power[:, :RADIX] + power[:, RADIX:]
        base = jnp.where(group == 0, both * (1.0 / GROUP), level[...])
        level[...] = base
        level_sum[...] += both
        for i in range(GROUP):
            at = pl.ds(pl.multiple_of((group * GROUP + i) * RADIX, RADIX), RADIX)
            centered[:, at] = (power[:, i * RADIX : (i + 1) * RADIX] - base).astype(BF16)
        at = pl.ds(pl.multiple_of(group * GROUP * RADIX, GROUP * RADIX), GROUP * RADIX)

        def add_rows(step, _):
            rows = pl.ds(pl.multiple_of(step * block_rows, block_rows), block_rows)
            series[rows, :] += lax.dot_general(hot[rows, at], centered[:, at], contract, preferred_element_type=F32)
            return 0

        lax.fori_loop(0, 2 * half_rows // block_rows, add_rows, 0)
        return 0

    last_group = SPECTRA // GROUP - 1
    lax.fori_loop(0, last_group, beamform, 0)

    def last_beams(t):
        beams = slice(t * RADIX, (t + 1) * RADIX)
        spectra = spectra_of(last_group)
        power = power_of(
            jnp.dot(steer[t * RADIX : (t + 1) * RADIX, :], spectra, preferred_element_type=F32),
            jnp.dot(steer[BEAMS + t * RADIX : BEAMS + (t + 1) * RADIX, :], spectra, preferred_element_type=F32),
        )
        base = level[beams, :]
        total = level_sum[beams, :] + power[:, :RADIX] + power[:, RADIX:]
        for i in range(GROUP):
            s = last_group * GROUP + i
            centered[beams, s * RADIX : (s + 1) * RADIX] = (power[:, i * RADIX : (i + 1) * RADIX] - base).astype(BF16)
        centered[beams, SPECTRA * RADIX :] = (base - total * (1.0 / SPECTRA)).astype(BF16)

    def last_rows(rows, t):
        at = slice(last_group * GROUP * RADIX, (SPECTRA + 1) * RADIX)
        beams = slice(t * RADIX, (t + 1) * RADIX)
        return series[rows, beams] + lax.dot_general(
            hot[rows, at], centered[beams, at], contract, preferred_element_type=F32
        )

    def pair_copy(t):
        return pltpu.make_async_remote_copy(
            src_ref=pair_send.at[t], dst_ref=pair_land.at[t], send_sem=pair_sems.at[0, t], recv_sem=pair_sems.at[1, t],
            device_id=other(here, (0, 0, 0), 1), device_id_type=MESH,
        )

    def owners_out(t):
        pair_copy(t).wait_recv()
        mine = series[0:half_rows, t * RADIX : (t + 1) * RADIX] + pair_land[t].astype(F32)
        owner_own[t] = mine[0:ROWS, :]
        owner_send[t] = mine[ROWS:, :].astype(BF16).reshape(CHIPS - 1, ROWS, RADIX)
        for i, offset in enumerate(CHIP_ORDER):
            pltpu.make_async_remote_copy(
                src_ref=owner_send.at[t, i], dst_ref=owner_land.at[t, i],
                send_sem=owner_sems.at[0, t], recv_sem=owner_sems.at[1, t],
                device_id=other(here, offset, 0), device_id_type=MESH,
            ).start()

    land(last_group)
    for t in range(TILES):
        last_beams(t)
        pair_send[t] = last_rows(slice(half_rows, 2 * half_rows), t).astype(BF16)
        pair_copy(t).start()
        series[0:half_rows, t * RADIX : (t + 1) * RADIX] = last_rows(slice(0, half_rows), t)
        owners_out(t)
    for t in range(TILES):
        pltpu.make_async_copy(owner_land.at[t], owner_land.at[t], owner_sems.at[1, t]).wait()
        totals = [owner_own[t], 0.0, 0.0, 0.0]
        for i in range(CHIPS - 1):
            totals[i % 4] += owner_land[t, i].astype(F32)
        total = (totals[0] + totals[1]) + (totals[2] + totals[3])
        for r in range(MOST_DM):
            out[r, :, t * RADIX : (t + 1) * RADIX] = total[r * OUT_T : (r + 1) * OUT_T, :]

    for t in range(TILES):
        pair_copy(t).wait_send()
        pltpu.make_async_copy(owner_send.at[t], owner_send.at[t], owner_sems.at[0, t]).wait()
    gone = sending.at[0 : DEVICES - 1]
    pltpu.make_async_copy(gone, gone, send_sem).wait()


def local(voltages, filter_weights, beam_delay_index, delays, dm_counts):
    dft, twist = tables()
    anywhere = pl.BlockSpec(memory_space=pl.ANY)
    return pl.pallas_call(
        body,
        out_shape=jax.ShapeDtypeStruct((MOST_DM, OUT_T, BEAMS), F32),
        in_specs=[anywhere] * 7,
        out_specs=pl.BlockSpec(memory_space=pltpu.VMEM),
        scratch_shapes=[
            pltpu.VMEM((FRAMES, 2, ANTENNAS, LENGTH), BF16),
            pltpu.VMEM((TAPS, LENGTH), F32),
            pltpu.VMEM((BEAMS, DEVICES * ANTENNAS), jnp.int32),
            pltpu.VMEM((TRIALS, RADIX), jnp.int32),
            pltpu.VMEM((1, DEVICES), jnp.int32),
            pltpu.VMEM((256, 768), BF16),
            pltpu.VMEM((256, RADIX), F32),
            pltpu.VMEM((2 * RADIX * ANTENNAS, RADIX), F32),
            pltpu.VMEM((ANTENNAS // 2, 512, 256), BF16),
            pltpu.VMEM((ANTENNAS // 2, 256, 512), BF16),
            pltpu.VMEM((2 * RADIX * ANTENNAS, RADIX), F32),
            pltpu.VMEM((DEVICES, SPECTRA, 2 * ANTENNAS, RADIX), BF16),
            pltpu.VMEM((DEVICES, SPECTRA, 2 * ANTENNAS, RADIX), BF16),
            pltpu.VMEM((2 * BEAMS, DEVICES * 2 * ANTENNAS), BF16),
            pltpu.VMEM((BEAMS, RADIX), F32),
            pltpu.VMEM((BEAMS, RADIX), F32),
            pltpu.VMEM((BEAMS, (SPECTRA + 1) * RADIX), BF16),
            pltpu.VMEM((DEVICES * ROWS, (SPECTRA + 1) * RADIX), BF16),
            pltpu.VMEM((DEVICES * ROWS, BEAMS), F32),
            pltpu.VMEM((TILES, CHIPS * ROWS, RADIX), BF16),
            pltpu.VMEM((TILES, CHIPS * ROWS, RADIX), BF16),
            pltpu.VMEM((TILES, ROWS, RADIX), F32),
            pltpu.VMEM((TILES, CHIPS - 1, ROWS, RADIX), BF16),
            pltpu.VMEM((TILES, CHIPS - 1, ROWS, RADIX), BF16),
            pltpu.SemaphoreType.DMA((FRAMES,)),
            pltpu.SemaphoreType.DMA((6,)),
            pltpu.SemaphoreType.DMA,
            pltpu.SemaphoreType.DMA((SPECTRA,)),
            pltpu.SemaphoreType.DMA((2, TILES)),
            pltpu.SemaphoreType.DMA((2, TILES)),
        ],
        compiler_params=pltpu.CompilerParams(
            collective_id=0, has_side_effects=True, vmem_limit_bytes=62 << 20
        ),
        cost_estimate=pl.CostEstimate(flops=16_000_000_000, bytes_accessed=12_000_000, transcendentals=0),
        name="channelize_turn_beamform",
    )(voltages, filter_weights, beam_delay_index, delays, dm_counts.reshape(1, DEVICES), dft, twist)


def solution(mesh):
    in_specs = (P(None, ("freq", "dm"), None), P(), P(), P(None, ("freq", "dm")), P())
    out_specs = P(("freq", "dm"), None, None)
    return jax.shard_map(local, mesh=mesh, in_specs=in_specs, out_specs=out_specs, check_vma=False)
```
